32 devices in a mesh: band: 4 (over z), lev: 8 (over y, x, core).
Axes of the slice: x: 2, y: 2, z: 4, core: 2. Of those that a mesh axis runs over, the one named last changes fastest.
Arguments:
- neutrals: float32 [5, 64, 32, 2880], P(None, 'lev', 'band'), may hold values from -6 to 6
- wind_lon: float32 [64, 32, 2880], P('lev', 'band'), may hold values from -0.15 to 0.15
- wind_lat: float32 [64, 32, 2880], P('lev', 'band'), may hold values from -0.15 to 0.15
- wind_lev: float32 [64, 32, 2880], P('lev', 'band'), may hold values from -0.15 to 0.15
- eddy_coupling: float32 [5, 64], replicated, may hold values from 0.3 to 6
- pair_weight: float32 [32, 32, 2880], P(None, 'band'), may hold values from 0 to 1
- ion_yield: float32 [7, 5], replicated, may hold values from -2.5 to 2.5
- ion_spread: float32 [7], replicated, may hold values from 0.02 to 0.4
- ion_loss: float32 [7], replicated, may hold values from 0.005 to 0.1
- column_order: int32 [4, 23040], P('band'), may hold values from 0 to 23039, each once within a row
- column_units: int32 [8], replicated, may hold values from 1 to 1080, 5760 in all
- tube_owner: int32 [8, 1080, 1], replicated, may hold values from 0 to 31; in each aligned block of 1080 rows (0 to 1079, 1080 to 2159, ..., all dimensions but the last counted through in order) at most 34 rows name the same one
Outputs:
- column_state: float32 [4, 8, 5, 64, 4320], P('band', 'lev')
- ion_lines: float32 [32, 272, 7, 512], P(('band', 'lev'))
The draws below stay inside these ranges and needn't reach their ends.
Inputs may be any that keep to these rules, and one draw needn't show every extreme that they name: `column_order`: each row lists every column of its band once. `column_units`: the counts sum to 5760; the largest is 1080. `tube_owner`: among the 1080 slots of one owner no tube owner is named more than 34 times, and some is named exactly that often.
All inputs are finite; a program needn't handle non-finite values.
Results may differ from the reference program's by a relative error of at most 0.0003.
Values sent between devices are 32-bit elements; how exact they have to be, the bound alone decides.
A program may use at most 320 MiB of HBM per device.

```python
import math
import jax
import jax.numpy as jnp
import numpy as np
from jax import lax

SPECIES = 5
IONS = 7
NLON = 2880
NLEV = 64
TUBE_COLS = 4
TSTEPS = 2
SWEEPS = 8
SECTIONS = 20
BANDS = 4
OWNERS = 8
PEERS = 32
NLAT = 32
COLS = 23040
BAND_TUBES = 5760
TUBE_CAP = 1080
COL_CAP = 4320
PEER_SLOTS = 34
PAIRS = 32
LINE_PTS = 512


def block_scale(own_key, shape, shards, least, top_value):
    level = 1.0
    for position, shards_of in shards:
        heights = jax.random.uniform(jax.random.fold_in(jax.random.fold_in(own_key, 6), position), (shards_of,), jnp.float32, least / len(shards), top_value / len(shards))
        level = level * jnp.repeat(jnp.exp(heights), shape[position] // shards_of).reshape((-1,) + (1,) * (len(shape) - 1 - position))
    return level


def split_up(count, total, limit, skew):
    portions = [(1 << 20) // math.isqrt(standing ** skew) + 1 for standing in range(2, count + 1)]
    surplus, counts = total - limit - (count - 1), [1] * (count - 1)
    while surplus > 0:
        candidates = [i for i in range(count - 1) if counts[i] < limit]
        pool, remaining = sum([portions[i] for i in candidates]), surplus
        for i in candidates:
            addition = min(limit - counts[i], max(1, remaining * portions[i] // pool), surplus)
            counts[i] = counts[i] + addition
            surplus = surplus - addition
    return np.array([limit] + counts)


def uneven_parts(stream_key, amount, total, reach, skew):
    if amount == 2:
        one = jax.random.randint(stream_key, (), max(1, total - reach), min(reach, total - 1) + 1)
        return jnp.stack([one, total - one])
    tallies = jnp.asarray(split_up(amount, total, reach, skew), jnp.int32)
    pairs = (amount - 1) // 2
    giver, taker = tallies[1:1 + 2 * pairs:2], tallies[2:2 + 2 * pairs:2]
    margin = jnp.minimum(giver - 1, reach - taker)
    shifted = jax.random.randint(jax.random.fold_in(stream_key, 1), (pairs,), 0, 1 << 20) % (margin + 1)
    tallies = tallies.at[1:1 + 2 * pairs:2].set(giver - shifted).at[2:2 + 2 * pairs:2].set(taker + shifted)
    return tallies[jax.random.permutation(jax.random.fold_in(stream_key, 2), amount)]


def deal_out(rng, own, number, rows, number_of, top, limit, skew):
    order = jax.random.permutation(rng, number_of)
    packed, common = load_shares(number_of, rows * top, limit, skew, True), load_shares(number_of, rows * top, limit, skew, False)
    places = jnp.arange(number_of)

    def named(lengths, rotation):
        used = int((lengths > 0).sum())
        fixed = max(1, used // 4)
        moved = fixed + (places - fixed + rotation * (used - fixed)) % max(1, number_of - fixed)
        return jnp.zeros((number_of,), jnp.int32).at[order[jnp.where(places < fixed, places, moved)]].set(jnp.asarray(lengths, jnp.int32))

    lengths = jnp.where(number % 4 == 0, named(packed, number // 4), named(common, number - number // 4 - 1))
    mixed = jax.random.permutation(jax.random.fold_in(own, 3), number_of)
    source_of, sink = mixed[0:number_of // 2 * 2:2], mixed[1:number_of // 2 * 2:2]
    margin = jnp.minimum(lengths[source_of] - 1, limit - lengths[sink]) // 2
    margin = jnp.where((source_of == order[0]) | (sink == order[0]) | (lengths[sink] == 0), 0, jnp.maximum(margin, 0))
    moved = jax.random.randint(jax.random.fold_in(own, 4), (number_of // 2,), 0, 1 << 20) % (margin + 1)
    lengths = lengths.at[source_of].add(-moved).at[sink].add(moved)
    labels = jnp.searchsorted(jnp.cumsum(lengths), jnp.arange(rows * top), side="right").astype(jnp.int32)
    listing = labels.reshape(top, rows).T
    listing = listing[jax.random.permutation(jax.random.fold_in(own, 1), rows)]
    rotation = jax.random.randint(jax.random.fold_in(own, 2), (rows, 1), 0, top)
    return jnp.take_along_axis(listing, (jnp.arange(top)[None, :] + rotation) % top, axis=1)


def load_shares(number_of, total, bound, slope, full):
    loads = [(1 << 20) // math.isqrt(standing ** slope) + 1 for standing in range(1, number_of + 1)]
    largest = bound if full else min(bound, max(-(-total // number_of), total * loads[0] // sum(loads)))
    least = 1 if total - largest >= number_of - 1 else 0
    counts, rest = [largest] + [least] * (number_of - 1), total - largest - least * (number_of - 1)
    while rest > 0:
        movable = [i for i in range(1, number_of) if counts[i] < largest] or [i for i in range(1, number_of) if counts[i] < bound]
        pool, budget = sum([loads[i] for i in movable]), rest
        for i in movable:
            more = min(bound - counts[i], max(1, budget * loads[i] // pool), rest)
            counts[i] = counts[i] + more
            rest = rest - more
    return np.array(counts)


def bell_draw(key, extent, scale, bound, shards=(), kind=jnp.bfloat16):
    values = scale * jax.random.normal(key, extent, jnp.float32)
    if shards:
        values = values * block_scale(key, extent, shards, -0.22, 0.18)
    return jnp.clip(values, -bound, bound).astype(kind)


def setup_inputs(seed: int = 0) -> dict:
    key_list = jax.random.split(jax.random.key(seed), 13)
    neutrals = bell_draw(key_list[0], (SPECIES, NLEV, NLAT, NLON), 1.0, 6.0, ((1, 8), (2, 4)), jnp.float32)
    wind_lon = jnp.clip(jax.random.uniform(key_list[1], (NLEV, NLAT, NLON), jnp.float32, -0.15, 0.15) * block_scale(key_list[1], (NLEV, NLAT, NLON), ((0, 8), (1, 4)), -0.4, 0.0), -0.15, 0.15)
    wind_lat = jnp.clip(jax.random.uniform(key_list[2], (NLEV, NLAT, NLON), jnp.float32, -0.15, 0.15) * block_scale(key_list[2], (NLEV, NLAT, NLON), ((0, 8), (1, 4)), -0.4, 0.0), -0.15, 0.15)
    wind_lev = jnp.clip(jax.random.uniform(key_list[3], (NLEV, NLAT, NLON), jnp.float32, -0.15, 0.15) * block_scale(key_list[3], (NLEV, NLAT, NLON), ((0, 8), (1, 4)), -0.4, 0.0), -0.15, 0.15)
    eddy_coupling = jnp.clip(jnp.exp(jax.random.uniform(key_list[4], (SPECIES, NLEV), jnp.float32, math.log(0.3), math.log(6.0))), 0.3, 6.0)
    pair_weight = jnp.clip(1.0 * jax.random.uniform(key_list[5], (PAIRS, NLAT, NLON), jnp.float32) ** block_scale(key_list[5], (PAIRS, NLAT, NLON), ((1, 4),), -0.2, 0.2), 0.0, 1.0)
    ion_yield = bell_draw(key_list[6], (IONS, SPECIES), SPECIES ** -0.5, 2.5, (), jnp.float32)
    ion_spread = jnp.clip(jnp.exp(jax.random.uniform(key_list[7], (IONS,), jnp.float32, math.log(0.02), math.log(0.4))), 0.02, 0.4)
    ion_loss = jnp.clip(jnp.exp(jax.random.uniform(key_list[8], (IONS,), jnp.float32, math.log(0.005), math.log(0.1))), 0.005, 0.1)
    column_order = jax.vmap(lambda own: jax.random.permutation(own, COLS))(jax.random.split(key_list[9], BANDS)).reshape((BANDS, COLS)).astype(jnp.int32)
    column_units = uneven_parts(key_list[10], OWNERS, BAND_TUBES, TUBE_CAP, 2).astype(jnp.int32)
    tube_owner_keys = jax.random.split(jax.random.fold_in(key_list[11], 1), OWNERS * TUBE_CAP // TUBE_CAP)
    tube_owner_turns = jax.random.permutation(jax.random.fold_in(key_list[11], 3), OWNERS * TUBE_CAP // TUBE_CAP)
    tube_owner = jax.vmap(lambda own, number: deal_out(jax.random.fold_in(key_list[11], 2), own, number, TUBE_CAP, PEERS, 1, PEER_SLOTS, 2))(tube_owner_keys, tube_owner_turns).reshape((OWNERS, TUBE_CAP, 1))
    return {"neutrals": neutrals, "wind_lon": wind_lon, "wind_lat": wind_lat, "wind_lev": wind_lev, "eddy_coupling": eddy_coupling, "pair_weight": pair_weight, "ion_yield": ion_yield, "ion_spread": ion_spread, "ion_loss": ion_loss, "column_order": column_order, "column_units": column_units, "tube_owner": tube_owner}


HIGHEST = lax.Precision.HIGHEST


def upwind_faces(courant, upstream, downstream):
    return jnp.maximum(courant, 0.0) * upstream + jnp.minimum(courant, 0.0) * downstream


def transport_once(density, wind_lon, wind_lat, wind_lev):
    western = jnp.roll(density, 1, axis=3)
    flux_lon = upwind_faces(wind_lon, western, density)
    change = flux_lon - jnp.roll(flux_lon, -1, axis=3)
    across = jnp.pad(density, ((0, 0), (0, 0), (1, 1), (0, 0)))
    courant = jnp.pad(wind_lat, ((0, 0), (1, 1), (0, 0)))
    flux_lat = upwind_faces(courant[:, 1:], across[:, :, :-1], across[:, :, 1:])
    change = change + flux_lat[:, :, :-1] - flux_lat[:, :, 1:]
    upward = jnp.pad(density, ((0, 0), (1, 1), (0, 0), (0, 0)))
    courant = jnp.pad(wind_lev, ((1, 1), (0, 0), (0, 0)))
    flux_lev = upwind_faces(courant[1:], upward[:, :-1], upward[:, 1:])
    change = change + flux_lev[:, :-1] - flux_lev[:, 1:]
    return density + change


def vertical_solve(density, eddy_coupling):
    zero_edge = jnp.zeros((eddy_coupling.shape[0], 1), jnp.float32)
    coupling_below = jnp.concatenate([zero_edge, eddy_coupling[:, 1:]], 1)[:, :, None]
    coupling_above = jnp.concatenate([eddy_coupling[:, 1:], zero_edge], 1)[:, :, None]
    diagonal = 1.0 + coupling_below + coupling_above
    iterate = density
    zero_layer = jnp.zeros_like(density[:, :1])
    for sweep_index in range(SWEEPS):
        beneath = jnp.concatenate([zero_layer, iterate[:, :-1]], 1)
        overhead = jnp.concatenate([iterate[:, 1:], zero_layer], 1)
        iterate = (density + coupling_below * beneath + coupling_above * overhead) / diagonal
    return iterate


def interpolate(ion_yield, neutral_block, weight_block):
    paired = weight_block * neutral_block[..., 0::2] + (1.0 - weight_block) * neutral_block[..., 1::2]
    return jnp.einsum("is,...scp->...icp", ion_yield, paired, precision=HIGHEST)


def line_diffusion(source, ion_spread, ion_loss):
    spread_rate = ion_spread[:, None]
    loss_rate = ion_loss[:, None]

    def advance(section_index, density):
        left_side = jnp.concatenate([density[..., :1], density[..., :-1]], -1)
        right_side = jnp.concatenate([density[..., 1:], density[..., -1:]], -1)
        return density + spread_rate * (left_side - 2.0 * density + right_side) + source - loss_rate * density

    return lax.fori_loop(0, SECTIONS, advance, jnp.zeros_like(source))


def owner_table(destinations):
    device_ids = jnp.arange(PEERS, dtype=jnp.int32)
    matches = (destinations[:, None] == device_ids[None, :]).astype(jnp.int32)
    rank_of = jnp.sum(jnp.cumsum(matches, 0) * matches, 1) - 1
    flat_slot = (destinations * PEER_SLOTS + rank_of).astype(jnp.int32)
    empty_table = jnp.full((PEERS * PEER_SLOTS,), TUBE_CAP, jnp.int32)
    return empty_table.at[flat_slot].set(jnp.arange(TUBE_CAP, dtype=jnp.int32))


def reference(neutrals, wind_lon, wind_lat, wind_lev, eddy_coupling, pair_weight, ion_yield, ion_spread, ion_loss, column_order, column_units, tube_owner):
    species = neutrals.shape[0]
    ion_count = ion_yield.shape[0]
    density = neutrals
    for substep in range(TSTEPS):
        density = transport_once(density, wind_lon, wind_lat, wind_lev)
    solved = vertical_solve(density.reshape(species, NLEV, NLAT * NLON), eddy_coupling)
    by_band = solved.reshape(species, NLEV, BANDS, COLS)
    starts = jnp.cumsum(column_units) - column_units
    slot_ids = jnp.arange(COL_CAP, dtype=jnp.int32)
    positions = jnp.minimum(TUBE_COLS * starts[:, None] + slot_ids[None, :], COLS - 1).astype(jnp.int32)
    live_slots = (slot_ids[None, :] < TUBE_COLS * column_units[:, None]).astype(jnp.float32)
    column_ids = column_order[:, positions]

    def band_columns(band_index):
        gathered = jnp.take(by_band[:, :, band_index], column_ids[band_index], axis=2)
        return jnp.transpose(gathered, (2, 0, 1, 3)) * live_slots[:, None, None, :]

    column_state = lax.map(band_columns, jnp.arange(BANDS, dtype=jnp.int32))
    weight_band = pair_weight.reshape(PAIRS, BANDS, COLS)

    def band_weights(band_index):
        return jnp.transpose(jnp.take(weight_band[:, band_index], column_ids[band_index], axis=1), (1, 0, 2))

    weight_state = lax.map(band_weights, jnp.arange(BANDS, dtype=jnp.int32))
    slot_table = jax.vmap(owner_table)(tube_owner[:, :, 0]).reshape(OWNERS, PEERS, PEER_SLOTS)
    state_blocks = column_state.reshape(BANDS, OWNERS, species, NLEV, TUBE_CAP, TUBE_COLS)
    weight_blocks = weight_state.reshape(BANDS, OWNERS, PAIRS, TUBE_CAP, TUBE_COLS)
    owner_ids = jnp.arange(OWNERS, dtype=jnp.int32)[:, None]

    def device_lines(device):
        picked = slot_table[:, device]
        alive_mask = (picked < column_units[:, None]).astype(jnp.float32)
        clipped = jnp.minimum(picked, TUBE_CAP - 1)
        neutral_part = state_blocks[:, owner_ids, :, :, clipped, :]
        neutral_part = jnp.swapaxes(neutral_part, 4, 5) * alive_mask[:, :, None, None, None, None]
        weight_part = jnp.swapaxes(weight_blocks[:, owner_ids, :, clipped, :], 3, 4)[:, :, :, None]
        sources = interpolate(ion_yield, neutral_part, weight_part)
        sources = jnp.transpose(sources, (0, 1, 3, 2, 4, 5)).reshape(OWNERS * PEER_SLOTS, ion_count, LINE_PTS)
        return line_diffusion(sources, ion_spread, ion_loss)

    ion_lines = lax.map(device_lines, jnp.arange(PEERS, dtype=jnp.int32))
    return column_state, ion_lines
```

```python
import functools

import jax
import jax.numpy as jnp
from jax import lax
from jax.experimental import pallas as pl
from jax.experimental.pallas import tpu as pltpu
from jax.sharding import PartitionSpec as P

NLEV = 64
TUBE_COLS = 4
TSTEPS = 2
SWEEPS = 8
SECTIONS = 20

LANES = 128
TILE_COLS = 256
VMEM_BYTES = 48 * 1024 * 1024


def from_above(cells, axis, dim):
    ends = lax.axis_size(axis) - 1
    head = lax.slice_in_dim(cells, 0, 1, axis=dim)
    return lax.ppermute(head, axis, [(i + 1, i) for i in range(ends)])


def from_below(cells, axis, dim):
    ends = lax.axis_size(axis) - 1
    tail = lax.slice_in_dim(cells, cells.shape[dim] - 1, cells.shape[dim], axis=dim)
    return lax.ppermute(tail, axis, [(i, i + 1) for i in range(ends)])


def upwind_faces(courant, upstream, downstream):
    return jnp.maximum(courant, 0.0) * upstream + jnp.minimum(courant, 0.0) * downstream


def transport_once(density, wind_lon, lat_faces, lev_faces):
    beside = [from_below(density, "band", 2), from_above(density, "band", 2)]
    stacked = [from_below(density, "lev", 1), from_above(density, "lev", 1)]
    western = jnp.roll(density, 1, axis=3)
    flux_lon = upwind_faces(wind_lon, western, density)
    change = flux_lon - jnp.roll(flux_lon, -1, axis=3)
    across = jnp.concatenate([beside[0], density, beside[1]], 2)
    flux_lat = upwind_faces(lat_faces, across[:, :, :-1], across[:, :, 1:])
    change = change + flux_lat[:, :, :-1] - flux_lat[:, :, 1:]
    upward = jnp.concatenate([stacked[0], density, stacked[1]], 1)
    flux_lev = upwind_faces(lev_faces, upward[:, :-1], upward[:, 1:])
    change = change + flux_lev[:, :-1] - flux_lev[:, 1:]
    return density + change


def round_up(count, multiple):
    return (count + multiple - 1) // multiple * multiple


def gather_kernel(lons, order_ref, start_ref, live_ref, grid_ref, out_ref, table, rows):
    owner = pl.program_id(0)
    lats, depth, padded_lons = grid_ref.shape

    @pl.when(owner == 0)
    def fill_table():
        def one_lat(lat, carry):
            for tile in range(padded_lons // LANES):
                block = grid_ref[lat, :, tile * LANES : (tile + 1) * LANES]
                at = pl.multiple_of(lat * lons + tile * LANES, 8)
                table[pl.ds(at, LANES), :depth] = block.T
            return carry

        lax.fori_loop(0, lats, one_lat, 0)

    out_ref[...] = jnp.zeros_like(out_ref)
    start = start_ref[owner]
    live = live_ref[owner]
    lane = lax.broadcasted_iota(jnp.int32, (depth, LANES), 1)

    def one_tile(tile, carry):
        base = start + tile * LANES
        for row in range(LANES):
            rows[pl.ds(row, 1), :] = table[pl.ds(order_ref[base + row], 1), :]
        block = rows[...].T[:depth]
        at = pl.multiple_of(tile * LANES, LANES)
        out_ref[0, :, pl.ds(at, LANES)] = jnp.where(lane < live - tile * LANES, block, 0.0)
        return carry

    lax.fori_loop(0, (live + LANES - 1) // LANES, one_tile, 0)


def gather_columns(density, order, starts, live, column_pad):
    species, levels, lats, lons = density.shape
    owners = starts.shape[0]
    depth = round_up(species * levels, 8)
    padded_lons = round_up(lons, LANES)
    by_lat = jnp.transpose(density.reshape(species * levels, lats, lons), (1, 0, 2))
    by_lat = jnp.pad(
        by_lat, ((0, 0), (0, depth - species * levels), (0, padded_lons - lons))
    )
    table_rows = (lats - 1) * lons + padded_lons
    return pl.pallas_call(
        functools.partial(gather_kernel, lons),
        grid_spec=pltpu.PrefetchScalarGridSpec(
            num_scalar_prefetch=3,
            grid=(owners,),
            in_specs=[pl.BlockSpec((lats, depth, padded_lons), lambda o, *_: (0, 0, 0))],
            out_specs=pl.BlockSpec((1, depth, column_pad), lambda o, *_: (o, 0, 0)),
            scratch_shapes=[
                pltpu.VMEM((table_rows, LANES), jnp.float32),
                pltpu.VMEM((LANES, LANES), jnp.float32),
            ],
        ),
        out_shape=jax.ShapeDtypeStruct((owners, depth, column_pad), jnp.float32),
        compiler_params=pltpu.CompilerParams(vmem_limit_bytes=VMEM_BYTES),
        name="gather_columns",
    )(order, starts, live, by_lat)


def solve_kernel(
    levels, in_ref, weight_ref, below_ref, above_ref, scale_ref, state_ref, tube_ref, solved, turned
):
    species = state_ref.shape[0]
    level_blocks = in_ref.shape[0]
    depth = state_ref.shape[1]
    pairs = depth // 2
    tubes = LANES // TUBE_COLS
    for tile in range(state_ref.shape[2] // LANES):
        lanes = slice(tile * LANES, (tile + 1) * LANES)
        weight = weight_ref[:, lanes]
        for kind in range(species):
            for part in range(level_blocks):
                solved[kind, part * levels : (part + 1) * levels, :] = in_ref[
                    part, kind * levels : (kind + 1) * levels, lanes
                ]
            iterate = solved[kind]
            scaled = iterate * scale_ref[kind]
            below, above = below_ref[kind], above_ref[kind]
            for sweep_index in range(SWEEPS):
                iterate = (
                    scaled
                    + below * pltpu.roll(iterate, 1, 0)
                    + above * pltpu.roll(iterate, depth - 1, 0)
                )
            solved[kind] = iterate
            state_ref[kind, :, lanes] = iterate
            lower = solved[kind, pl.ds(0, pairs, stride=2), :]
            upper = solved[kind, pl.ds(1, pairs, stride=2), :]
            turned[kind] = (weight * lower + (1.0 - weight) * upper).T
            row = jnp.concatenate(
                [turned[kind, pl.ds(c, tubes, stride=TUBE_COLS), :] for c in range(TUBE_COLS)], 1
            )
            segment = TUBE_COLS * pairs
            tube_ref[tile * tubes : (tile + 1) * tubes, kind * segment : (kind + 1) * segment] = row


def solve_columns(incoming, weights, eddy_coupling, column_slots, levels):
    level_blocks, depth, column_pad = incoming.shape
    species = eddy_coupling.shape[0]
    zero_edge = jnp.zeros((species, 1), jnp.float32)
    below = jnp.concatenate([zero_edge, eddy_coupling[:, 1:]], 1)
    above = jnp.concatenate([eddy_coupling[:, 1:], zero_edge], 1)
    scale = 1.0 / (1.0 + below + above)
    factors = [
        jnp.broadcast_to(factor[:, :, None], (species, NLEV, LANES))
        for factor in (below * scale, above * scale, scale)
    ]
    factor_spec = pl.BlockSpec((species, NLEV, LANES), lambda t: (0, 0, 0))
    pairs = NLEV // 2
    width = species * TUBE_COLS * pairs
    return pl.pallas_call(
        functools.partial(solve_kernel, levels),
        grid=(column_pad // TILE_COLS,),
        in_specs=[
            pl.BlockSpec((level_blocks, depth, TILE_COLS), lambda t: (0, 0, t)),
            pl.BlockSpec((pairs, TILE_COLS), lambda t: (0, t)),
            factor_spec,
            factor_spec,
            factor_spec,
        ],
        out_specs=[
            pl.BlockSpec((species, NLEV, TILE_COLS), lambda t: (0, 0, t)),
            pl.BlockSpec((TILE_COLS // TUBE_COLS, width), lambda t: (t, 0)),
        ],
        out_shape=[
            jax.ShapeDtypeStruct((species, NLEV, column_slots), jnp.float32),
            jax.ShapeDtypeStruct((column_pad // TUBE_COLS, width), jnp.float32),
        ],
        scratch_shapes=[
            pltpu.VMEM((species, NLEV, LANES), jnp.float32),
            pltpu.VMEM((species, LANES, pairs), jnp.float32),
        ],
        compiler_params=pltpu.CompilerParams(vmem_limit_bytes=VMEM_BYTES),
        name="solve_columns",
    )(incoming, weights, *factors)


def line_kernel(group, in_ref, yield_ref, spread_ref, centre_ref, out_ref, rows):
    bands, owners, items, width = in_ref.shape
    ions, lines, points = out_ref.shape
    segment = points // bands
    species = width // segment
    for owner in range(owners):
        rows[:, owner * items : (owner + 1) * items, :] = in_ref[:, owner]
    lane = lax.broadcasted_iota(jnp.int32, (8, segment), 1)
    is_first, is_last = lane == 0, lane == segment - 1

    def sides(pieces):
        before = [pltpu.roll(piece, 1, 1) for piece in pieces]
        after = [pltpu.roll(piece, segment - 1, 1) for piece in pieces]
        for band in range(bands):
            left = before[band - 1] if band else pieces[0]
            right = after[band + 1] if band + 1 < bands else pieces[-1]
            yield jnp.where(is_first, left, before[band]) + jnp.where(is_last, right, after[band])

    def one_block(block, carry):
        at = pl.multiple_of(block * 8, 8)
        for first in range(0, ions, group):
            kinds = range(first, min(first + group, ions))
            sources = []
            for ion in kinds:
                for band in range(bands):
                    total = None
                    for kind in range(species):
                        row = rows[band, pl.ds(at, 8), kind * segment : (kind + 1) * segment]
                        term = yield_ref[ion, kind] * row
                        total = term if total is None else total + term
                    sources.append(total)

            def advance(section_index, states):
                following = []
                for place, ion in enumerate(kinds):
                    own = slice(place * bands, (place + 1) * bands)
                    for state, source, side in zip(states[own], sources[own], sides(states[own])):
                        following.append(
                            (source + centre_ref[ion] * state) + spread_ref[ion] * side
                        )
                return tuple(following)

            states = lax.fori_loop(1, SECTIONS, advance, tuple(sources))
            for place, ion in enumerate(kinds):
                for band in range(bands):
                    out_ref[ion, pl.ds(at, 8), band * segment : (band + 1) * segment] = states[
                        place * bands + band
                    ]
        return carry

    lax.fori_loop(0, lines // 8, one_block, 0)


def line_diffusion(received, ion_yield, ion_spread, ion_loss):
    bands, owners, items, width = received.shape
    ions, species = ion_yield.shape
    points = bands * width // species
    whole = pl.BlockSpec(memory_space=pltpu.VMEM)
    scalars = pl.BlockSpec(memory_space=pltpu.SMEM)
    lines = pl.pallas_call(
        functools.partial(line_kernel, 4),
        in_specs=[whole, scalars, scalars, scalars],
        out_specs=whole,
        out_shape=jax.ShapeDtypeStruct((ions, owners * items, points), jnp.float32),
        scratch_shapes=[pltpu.VMEM((bands, owners * items, width), jnp.float32)],
        compiler_params=pltpu.CompilerParams(vmem_limit_bytes=VMEM_BYTES),
        name="line_diffusion",
    )(received, ion_yield, ion_spread, 1.0 - 2.0 * ion_spread - ion_loss)
    return jnp.transpose(lines, (1, 0, 2))


def on_device(
    neutrals,
    wind_lon,
    wind_lat,
    wind_lev,
    eddy_coupling,
    pair_weight,
    ion_yield,
    ion_spread,
    ion_loss,
    column_order,
    column_units,
    tube_owner,
):
    species = neutrals.shape[0]
    density = neutrals
    lat_faces = jnp.concatenate([wind_lat, from_above(wind_lat, "band", 1)], 1)
    lev_faces = jnp.concatenate([wind_lev, from_above(wind_lev, "lev", 0)], 0)
    for substep in range(TSTEPS):
        density = transport_once(density, wind_lon, lat_faces, lev_faces)
    owners = lax.axis_size("lev")
    band_count = lax.axis_size("band")
    peer_count = owners * band_count
    band_columns = density.shape[2] * density.shape[3]
    tube_slots = tube_owner.shape[1]
    column_slots = tube_slots * TUBE_COLS
    slot_most = max(2, (tube_slots + peer_count - 1) // peer_count)
    pair_count = NLEV // 2
    column_pad = round_up(column_slots + 1, TILE_COLS)
    starts = TUBE_COLS * (jnp.cumsum(column_units) - column_units)
    live = TUBE_COLS * column_units
    order = jnp.concatenate([column_order[0], jnp.zeros((column_pad,), jnp.int32)])
    outgoing = gather_columns(density, order, starts, live, column_pad)
    incoming = lax.all_to_all(outgoing, "lev", split_axis=0, concat_axis=0, tiled=True)
    owner_index = lax.axis_index("lev")
    own_ids = lax.dynamic_slice(order, (starts[owner_index],), (column_pad,))
    own_weights = jnp.take(
        pair_weight.reshape(pair_count, band_columns), own_ids, axis=1, mode="clip"
    )
    columns, tube_rows = solve_columns(
        incoming, own_weights, eddy_coupling, column_slots, density.shape[1]
    )
    destinations = tube_owner[owner_index, :, 0]
    device_ids = jnp.arange(peer_count, dtype=jnp.int32)
    matches = (destinations[:, None] == device_ids[None, :]).astype(jnp.int32)
    rank_of = jnp.sum(jnp.cumsum(matches, 0) * matches, 1) - 1
    empty_table = jnp.full((peer_count * slot_most,), tube_slots, jnp.int32)
    sources_of = empty_table.at[destinations * slot_most + rank_of].set(
        jnp.arange(tube_slots, dtype=jnp.int32)
    )
    outgoing_tubes = tube_rows.at[sources_of].get(mode="clip")
    row_width = tube_rows.shape[1]
    received = lax.all_to_all(
        outgoing_tubes.reshape(peer_count, slot_most, row_width),
        ("band", "lev"),
        split_axis=0,
        concat_axis=0,
        tiled=True,
    )
    lines = line_diffusion(
        received.reshape(band_count, owners, slot_most, row_width), ion_yield, ion_spread, ion_loss
    )
    column_state = columns.reshape(1, 1, species, NLEV, column_slots)
    return (column_state, lines[None])


def solution(mesh):
    placed = (
        P(None, "lev", "band", None),
        P("lev", "band", None),
        P("lev", "band", None),
        P("lev", "band", None),
        P(),
        P(None, "band", None),
        P(),
        P(),
        P(),
        P("band", None),
        P(),
        P(),
    )
    return jax.shard_map(
        on_device,
        mesh=mesh,
        in_specs=placed,
        out_specs=(P("band", "lev", None, None, None), P(("band", "lev"), None, None, None)),
        check_vma=False,
    )
```
